32 devices in a mesh: rep: 2 (over x), fsdp: 16 (over z, y, core).
Axes of the slice: x: 2, y: 2, z: 4, core: 2. Of those that a mesh axis runs over, the one named last changes fastest.
Arguments:
- hidden: bfloat16 [8192, 4096], P(('rep', 'fsdp')), may hold values from -6 to 6
- weight: bfloat16 [512, 4096], P('fsdp'), may hold values from -0.09375 to 0.09375
- adapter_a: float32 [4096, 128], P('fsdp'), may hold values from -0.09375 to 0.09375
- adapter_b: float32 [512, 128], P('fsdp'), may hold values from -0.25 to 0.25
- grad_a: float32 [2, 4096, 128], P('rep', 'fsdp'), may hold values from -0.09375 to 0.09375
- grad_b: float32 [2, 512, 128], P('rep', 'fsdp'), may hold values from -0.25 to 0.25
Outputs:
- projected: bfloat16 [8192, 512], P(('rep', 'fsdp'))
- merged: bfloat16 [512, 4096], P('fsdp')
The draws below stay inside these ranges and needn't reach their ends.
All inputs are finite; a program needn't handle non-finite values.
Results may differ from the reference program's by a relative error of at most 0.0049.
Values may be sent and summed in bfloat16 or wider, within the bound.
No kernel may reach another device: no remote copies, remote signals or barrier semaphores. Data moves between devices by JAX's collectives and lax.ppermute only.
A program may use at most 64 MiB of HBM per device.

```python
import jax
import jax.numpy as jnp
from jax import lax

IN = 4096
OUT = 512
RANK = 128
TOKENS = 8192
N_REP = 2


def levels(stream_key, shape, shards, smallest, largest):
    factor_of, own = 1.0, jax.random.fold_in(stream_key, 6)
    for axis_at, parts in shards:
        steps = jnp.exp(jax.random.uniform(jax.random.fold_in(own, axis_at), (parts,), jnp.float32, smallest / len(shards), largest / len(shards)))
        factor_of = factor_of * jnp.repeat(steps, shape[axis_at] // parts).reshape([-1 if axis == axis_at else 1 for axis in range(len(shape))])
    return factor_of


def centred(rng, extent, spread, bound, shards=(), dtype=jnp.bfloat16):
    values = spread * jax.random.normal(rng, extent, jnp.float32)
    if shards:
        values = values * levels(rng, extent, shards, -0.22, 0.18)
    return jnp.clip(values, -bound, bound).astype(dtype)


def setup_inputs(seed: int = 0) -> dict:
    key_list = jax.random.split(jax.random.key(seed), 7)
    return {
        "hidden": centred(key_list[0], (TOKENS, IN), 1.0, 6.0, ((0, 32),)),
        "weight": centred(key_list[1], (OUT, IN), IN ** -0.5, 0.09375, ((0, 16),)),
        "adapter_a": centred(key_list[2], (IN, RANK), IN ** -0.5, 0.09375, ((0, 16),), jnp.float32),
        "adapter_b": centred(key_list[3], (OUT, RANK), 0.045, 0.25, ((0, 16),), jnp.float32),
        "grad_a": centred(key_list[4], (N_REP, IN, RANK), 0.0156, 0.09375, ((0, 2), (1, 16)), jnp.float32),
        "grad_b": centred(key_list[5], (N_REP, OUT, RANK), 0.045, 0.25, ((0, 2), (1, 16)), jnp.float32),
    }


step_size = 0.5


def reference(hidden, weight, adapter_a, adapter_b, grad_a, grad_b):
    mean_a = jnp.sum(grad_a, axis=0) / N_REP
    mean_b = jnp.sum(grad_b, axis=0) / N_REP
    new_a = adapter_a - step_size * mean_a
    new_b = adapter_b - step_size * mean_b
    delta = lax.dot_general(new_b, new_a, (((1,), (1,)), ((), ())), precision=lax.Precision.HIGHEST, preferred_element_type=jnp.float32)
    merged = (weight.astype(jnp.float32) + delta).astype(jnp.bfloat16)
    projected = lax.dot_general(hidden, merged, (((1,), (1,)), ((), ())), preferred_element_type=jnp.float32)
    return projected.astype(jnp.bfloat16), merged
```

```python
import functools

import jax
import jax.numpy as jnp
from jax import lax
from jax.experimental import pallas as pl
from jax.experimental.pallas import tpu as pltpu
from jax.sharding import PartitionSpec as P

step_size = 0.5
AXES = ("rep", "fsdp")
NT = (((1,), (1,)), ((), ()))
NN = (((1,), (0,)), ((), ()))


def permute(rows, group, flip_rep, flip_fsdp):
    reps, shards = group
    pairs = [
        (r * shards + f, (r ^ flip_rep) * shards + (f ^ flip_fsdp))
        for r in range(reps)
        for f in range(shards)
    ]
    return lax.ppermute(rows, AXES, pairs)


def dot(a, b, dims):
    return lax.dot_general(a, b, dims, preferred_element_type=jnp.float32)


def general(hidden, weight, adapter_a, adapter_b, grad_a, grad_b):
    replicas = lax.axis_size("rep")
    summed = lax.psum((grad_a[0], grad_b[0]), "rep")
    new_a = adapter_a - step_size * (summed[0] / replicas)
    new_b = adapter_b - step_size * (summed[1] / replicas)
    full_a = lax.all_gather(new_a, "fsdp", axis=0, tiled=True)
    delta = lax.dot_general(new_b, full_a, NT, precision=lax.Precision.HIGHEST, preferred_element_type=jnp.float32)
    own_rows = (weight.astype(jnp.float32) + delta).astype(jnp.bfloat16)
    output = dot(hidden, lax.all_gather(own_rows, "fsdp", axis=0, tiled=True), NT)
    return output.astype(jnp.bfloat16), own_rows


def project_kernel(pieces, planes, *refs):
    n_w = len(pieces)
    w_refs, rest = refs[:n_w], refs[n_w:]
    ab_refs, rest = rest[:8], rest[8:]
    h_ref, hs_ref, own_ref, sib_ref, merged_ref = rest[:5]
    w_all, a_all, b_all, h_all, b_own, sems = rest[5:]
    x, f = lax.axis_index("rep"), lax.axis_index("fsdp")
    core = f & 1
    place = f >> 1
    half_w = w_all.shape[0] // (2 * 2 * planes)
    half_a = a_all.shape[0] // (4 * 2 * planes)
    half_b = half_w
    tokens = h_ref.shape[0]

    copies_h, copies_w, copies_a = [], [], []

    def copy(group, source, target):
        sem = sems.at[len(copies_h) + len(copies_w) + len(copies_a)]
        group.append(pltpu.make_async_copy(source, target, sem))

    copy(copies_h, h_ref, h_all.at[pl.ds(0, tokens)])
    copy(copies_h, hs_ref, h_all.at[pl.ds(tokens, tokens)])
    for ref, (dz, dy, dh) in zip(w_refs, pieces):
        at = place ^ (dz * 2 + dy)
        if dh is None:
            start, size = at * (2 * half_w), 2 * half_w
        else:
            start, size = at * (2 * half_w) + (x ^ dh) * half_w, half_w
        copy(copies_w, ref, w_all.at[pl.ds(pl.multiple_of(start, size), size)])
    for i, ref in enumerate(ab_refs):
        other, dy, dh = i // 4, (i % 4) // 2, i % 2
        for dz in range(planes):
            at = place ^ (dz * 2 + dy)
            row = dz * (half_a + half_b)
            shard = at * 2 + (core ^ other)
            start = pl.multiple_of(shard * (2 * half_a) + (x ^ dh) * half_a, half_a)
            copy(copies_a, ref.at[pl.ds(row, half_a)], a_all.at[pl.ds(start, half_a)])
            if not other:
                start = pl.multiple_of(at * (2 * half_b) + (x ^ dh) * half_b, half_b)
                copy(copies_a, ref.at[pl.ds(row + half_a, half_b)], b_all.at[pl.ds(start, half_b)])
    for c in copies_h + copies_w + copies_a:
        c.start()
    for c in copies_h:
        c.wait()
    for c in copies_a:
        c.wait()
    t = dot(h_all[...], a_all[...], NN)
    t_high = t.astype(jnp.bfloat16)
    t_low = (t - t_high.astype(jnp.float32)).astype(jnp.bfloat16)
    low = dot(t_high, b_all[...], NT) + dot(t_low, b_all[...], NT)
    for c in copies_w:
        c.wait()
    mine = pl.ds(pl.multiple_of(place * (2 * half_w), 2 * half_w), 2 * half_w)
    b_own[...] = b_all[mine, :]
    merged_ref[...] = (w_all[mine, :].astype(jnp.float32) + dot(b_own[...], a_all[...], NT)).astype(jnp.bfloat16)
    out = (dot(h_all[...], w_all[...], NT) + low).astype(jnp.bfloat16)
    own_ref[...] = out[:tokens]
    sib_ref[...] = out[tokens:]


def join_kernel(block, own_ref, other_ref, out_ref):
    core = lax.axis_index("fsdp") & 1
    n, m = own_ref.shape[1], out_ref.shape[1]
    source = lax.broadcasted_iota(jnp.int32, (n, m), 0)
    target = lax.broadcasted_iota(jnp.int32, (n, m), 1)
    base = (source // block) * (2 * block) + source % block
    here = (target == base + core * block).astype(jnp.bfloat16)
    there = (target == base + (1 - core) * block).astype(jnp.bfloat16)
    out_ref[...] = (dot(own_ref[...], here, NN) + dot(other_ref[...], there, NN)).astype(jnp.bfloat16)


def paired(hidden, weight, adapter_a, adapter_b, grad_a, grad_b):
    group = (lax.axis_size("rep"), lax.axis_size("fsdp"))
    planes = group[1] // 4
    x = lax.axis_index("rep")
    tokens, depth = hidden.shape
    rank = adapter_a.shape[1]
    ra, rb, rw = adapter_a.shape[0] // 2, adapter_b.shape[0] // 2, weight.shape[0] // 2

    def send(rows, dx=0, dz=0, dy=0, dc=0):
        return permute(rows, group, dx, dz * 4 + dy * 2 + dc)

    def half(rows, size, which):
        return lax.dynamic_slice_in_dim(rows, which * size, size, 0)

    grads = jnp.concatenate([half(grad_a[0], ra, 1 - x), half(grad_b[0], rb, 1 - x)])
    other = send(grads, dx=1)

    w_half = half(weight, rw, x)
    far = send(w_half, dz=2)
    near = send(w_half, dz=1)
    beside = send(weight, dy=1)
    sibling_hidden = send(hidden, dc=1)

    own = jnp.concatenate([half(grad_a[0], ra, x), half(grad_b[0], rb, x)])
    old = jnp.concatenate([half(adapter_a, ra, x), half(adapter_b, rb, x)])
    ab = (old - step_size * ((own + other) / group[0])).astype(jnp.bfloat16)
    ab_z = [ab] + [send(ab, dz=d) for d in range(1, planes)]

    w = {(0, 0, None): weight, (2, 0, 0): far, (1, 0, 0): near, (0, 1, None): beside}
    w[1, 0, 1] = send(near, dx=1)
    w[2, 0, 1] = send(far, dx=1)
    w[2, 1, 0] = send(far, dy=1)
    w[3, 0, 0] = send(far, dz=1)
    w[1, 1, None] = send(beside, dz=1)

    ab_00 = jnp.concatenate(ab_z)
    ab_01 = send(ab_00, dx=1)
    ab_10 = send(ab_00, dy=1)
    w[3, 0, 1] = send(w[3, 0, 0], dx=1)
    w[3, 1, 0] = send(w[3, 0, 0], dy=1)
    w[2, 1, 1] = send(w[2, 1, 0], dx=1)
    ab_11 = send(ab_01, dy=1)
    w[3, 1, 1] = send(w[3, 1, 0], dx=1)
    ab_c = [ab_00, ab_01, ab_10, ab_11]
    ab_c = ab_c + [send(v, dc=1) for v in ab_c]

    pieces = tuple(w)
    any_space = pl.BlockSpec(memory_space=pl.ANY)
    vmem = pl.BlockSpec(memory_space=pltpu.VMEM)
    columns = weight.shape[0] * group[1] // 2
    n_in = len(pieces) + len(ab_c) + 2
    half_out, half_sib, merged = pl.pallas_call(
        functools.partial(project_kernel, pieces, planes),
        out_shape=(
            jax.ShapeDtypeStruct((tokens, columns), jnp.bfloat16),
            jax.ShapeDtypeStruct((tokens, columns), jnp.bfloat16),
            jax.ShapeDtypeStruct(weight.shape, jnp.bfloat16),
        ),
        in_specs=[any_space] * n_in,
        out_specs=(vmem, vmem, vmem),
        scratch_shapes=[
            pltpu.VMEM((columns, depth), jnp.bfloat16),
            pltpu.VMEM((depth, rank), jnp.bfloat16),
            pltpu.VMEM((columns, rank), jnp.bfloat16),
            pltpu.VMEM((2 * tokens, depth), jnp.bfloat16),
            pltpu.VMEM((2 * rb, rank), jnp.bfloat16),
            pltpu.SemaphoreType.DMA((2 + len(pieces) + 12 * planes,)),
        ],
        compiler_params=pltpu.CompilerParams(vmem_limit_bytes=32 * 1024 * 1024),
        name="project",
    )(*[w[p] for p in pieces], *ab_c, hidden, sibling_hidden)
    received = send(half_sib, dc=1)
    projected = pl.pallas_call(
        functools.partial(join_kernel, weight.shape[0]),
        out_shape=jax.ShapeDtypeStruct((tokens, 2 * columns), jnp.bfloat16),
        in_specs=[vmem, vmem],
        out_specs=vmem,
        name="join",
    )(half_out, received)
    return projected, merged


def solution(mesh):
    paired_fits = mesh.shape["rep"] == 2 and mesh.shape["fsdp"] == 16
    return jax.shard_map(
        paired if paired_fits else general,
        mesh=mesh,
        in_specs=(
            P(("rep", "fsdp"), None),
            P("fsdp", None),
            P("fsdp", None),
            P("fsdp", None),
            P("rep", "fsdp", None),
            P("rep", "fsdp", None),
        ),
        out_specs=(P(("rep", "fsdp"), None), P("fsdp", None)),
        check_vma=False,
    )
```

```python
import functools

import jax
import jax.numpy as jnp
from jax import lax
from jax.experimental import pallas as pl
from jax.experimental.pallas import tpu as pltpu
from jax.sharding import PartitionSpec as P

step_size = 0.5
AXES = ("rep", "fsdp")
NT = (((1,), (1,)), ((), ()))
NN = (((1,), (0,)), ((), ()))
VMEM_LIMIT = 16 * 1024 * 1024
WIDE_LIMIT = 58 * 1024 * 1024
S_FLOPS = 4e9
U_FLOPS = 4e9
W_FLOPS = 1
M_FLOPS = 1


def dot(a, b, dims):
    return lax.dot_general(a, b, dims, preferred_element_type=jnp.float32)


def general(hidden, weight, adapter_a, adapter_b, grad_a, grad_b):
    replicas = lax.axis_size("rep")
    summed = lax.psum((grad_a[0], grad_b[0]), "rep")
    new_a = adapter_a - step_size * (summed[0] / replicas)
    new_b = adapter_b - step_size * (summed[1] / replicas)
    full_a = lax.all_gather(new_a, "fsdp", axis=0, tiled=True)
    delta = lax.dot_general(new_b, full_a, NT, precision=lax.Precision.HIGHEST, preferred_element_type=jnp.float32)
    own_rows = (weight.astype(jnp.float32) + delta).astype(jnp.bfloat16)
    output = dot(hidden, lax.all_gather(own_rows, "fsdp", axis=0, tiled=True), NT)
    return output.astype(jnp.bfloat16), own_rows


CORE, Y, Z1, Z2 = (0, 1), (0, 2), (0, 4), (0, 8)
REPLICA, X = (1, 0), (1, 1)


def send(rows, group, move, other_move=None, name="sent"):
    reps, shards = group
    pairs = []
    for r in range(reps):
        for f in range(shards):
            dr, df = move if (f & 1) == r or other_move is None else other_move
            pairs.append((r * shards + f, (r ^ dr) * shards + (f ^ df)))
    with jax.named_scope(name):
        return lax.ppermute(rows, AXES, pairs)


HELD = (
    ((0, 0, 0), (0, 0, 1)),
    ((2, 0, 0), (1, 0, 1)),
    ((0, 1, 0), (0, 1, 1)),
    ((2, 0, 1), (1, 0, 0)),
    ((2, 1, 0), (1, 1, 1)),
    ((3, 0, 0), (3, 0, 1)),
    ((2, 1, 1), (1, 1, 0)),
    ((3, 1, 0), (3, 1, 1)),
)
SHARDS = (((0, 0), (2, 0)), ((1, 0), (3, 0)), ((0, 1), (2, 1)), ((1, 1), (3, 1)))


def position():
    x, f = lax.axis_index("rep"), lax.axis_index("fsdp")
    return x, f >> 1, f & 1


def flips_of(i, kind):
    first, second = HELD[i]
    return [a + kind * (b - a) for a, b in zip(first, second)]


def shard_of(flips):
    x, place, _ = position()
    return (place ^ (flips[0] * 2 + flips[1])) * 2 + (x ^ flips[2])


def update_kernel(replicas, old_ref, own_ref, oa_ref, ob_ref, ab_ref):
    rows_a = oa_ref.shape[1]
    ab_ref[:rows_a] = (old_ref[:rows_a] - step_size * ((own_ref[:rows_a] + oa_ref[0]) / replicas)).astype(jnp.bfloat16)
    ab_ref[rows_a:] = (old_ref[rows_a:] - step_size * ((own_ref[rows_a:] + ob_ref[0]) / replicas)).astype(jnp.bfloat16)


def weight_kernel(h_ref, hs_ref, *refs):
    *shard_refs, own_ref, other_ref, w_all = refs
    rows = shard_refs[0].shape[0]
    for i, ref in enumerate(shard_refs):
        w_all[i * rows : (i + 1) * rows] = ref[...]
    other_ref[...] = dot(hs_ref[...], w_all[...], NT)
    own_ref[...] = dot(h_ref[...], w_all[...], NT)


def placing(rows, n, m, kind):
    source = lax.broadcasted_iota(jnp.int32, (n, m), 0)
    target = lax.broadcasted_iota(jnp.int32, (n, m), 1)
    column = jnp.zeros((n, m), jnp.int32)
    for i in range(len(HELD)):
        shard = shard_of(flips_of(i, kind))
        column = jnp.where(source // rows == i, shard * rows, column)
    return (target == column + source % rows).astype(jnp.bfloat16)


def split_bf16(v):
    high = v.astype(jnp.bfloat16)
    return high, (v - high.astype(jnp.float32)).astype(jnp.bfloat16)


def add_blocks(h_ref, w_ref, b_own, merged_ref, b_all, blocks, t):
    x, place, core = position()
    rows_b = w_ref.shape[0]
    rows_a = h_ref.shape[1] * rows_b // b_all.shape[0]
    for ref, other, at in blocks:
        for j, (dz, dy) in enumerate(SHARDS[at]):
            shard = (place ^ (dz * 2 + dy)) * 2 + (core ^ other)
            row = j * (rows_a + rows_b)
            columns = pl.ds(pl.multiple_of(shard * rows_a, rows_a), rows_a)
            part = ref[row : row + rows_a]
            b_all[pl.ds(pl.multiple_of(shard * rows_b, rows_b), rows_b)] = ref[row + rows_a : row + rows_a + rows_b]
            t = t + dot(h_ref[:, columns], part, NN)
            merged_ref[:, columns] = (w_ref[:, columns].astype(jnp.float32) + dot(b_own, part, NT)).astype(jnp.bfloat16)
    return t


def middle_kernel(at, h_ref, w_ref, *refs):
    *ab_refs, t_ref, merged_ref, b_all = refs
    rows_b = w_ref.shape[0]
    rows_a = h_ref.shape[1] * rows_b // b_all.shape[0]
    b_own = ab_refs[0][rows_a : rows_a + rows_b]
    blocks = [(ref, i // len(at), at[i % len(at)]) for i, ref in enumerate(ab_refs)]
    t_ref[...] = add_blocks(h_ref, w_ref, b_own, merged_ref, b_all, blocks, jnp.zeros(t_ref.shape, jnp.float32))


def last_kernel(at, h_ref, w_ref, own_ref, received_ref, t_ref, m_ref, b_ref, first_ref, *refs):
    *ab_refs, out_ref, merged_ref, b_all = refs
    x, place, core = position()
    kind = core ^ x
    n, m = own_ref.shape[1], out_ref.shape[1]
    rows_b = w_ref.shape[0]
    rows_a = h_ref.shape[1] * rows_b // b_all.shape[0]
    b_own = first_ref[rows_a : rows_a + rows_b]
    merged_ref[...] = m_ref[...]
    b_all[...] = b_ref[...]
    blocks = [(ref, i // len(at), at[i % len(at)]) for i, ref in enumerate(ab_refs)]
    t = add_blocks(h_ref, w_ref, b_own, merged_ref, b_all, blocks, t_ref[...])
    out = jnp.zeros(out_ref.shape, jnp.float32)
    for part in split_bf16(t):
        out = out + dot(part, b_all[...], NT)
    for ref, which in ((own_ref, kind), (received_ref, 1 - kind)):
        columns = placing(rows_b, n, m, which)
        for part in split_bf16(ref[...]):
            out = out + dot(part, columns, NN)
    out_ref[...] = out.astype(jnp.bfloat16)


def cost(flops, number_of_bytes):
    return pl.CostEstimate(flops=int(flops), bytes_accessed=int(number_of_bytes), transcendentals=0)


def paired(hidden, weight, adapter_a, adapter_b, grad_a, grad_b):
    group = (lax.axis_size("rep"), lax.axis_size("fsdp"))
    tokens, depth = hidden.shape
    rank = adapter_a.shape[1]
    rows_a, rows_b = adapter_a.shape[0], weight.shape[0]
    outputs = rows_b * group[1]

    any_space = pl.BlockSpec(memory_space=pltpu.HBM)
    vmem = pl.BlockSpec(memory_space=pltpu.VMEM)
    params = pltpu.CompilerParams(vmem_limit_bytes=VMEM_LIMIT)
    wide = pltpu.CompilerParams(vmem_limit_bytes=WIDE_LIMIT)
    bf16, f32 = jnp.bfloat16, jnp.float32

    w0 = weight
    other_a = send(grad_a, group, REPLICA, name="other_a")
    other_b = send(grad_b, group, REPLICA, name="other_b")
    w1 = send(w0, group, Z2, Z1, name="w1")
    w2 = send(w0, group, Y, name="w2")
    w1, w2 = lax.optimization_barrier((w1, w2))
    other_hidden = send(hidden, group, CORE, name="other_hidden")
    old, mine = lax.optimization_barrier((jnp.concatenate([adapter_a, adapter_b]), jnp.concatenate([grad_a[0], grad_b[0]])))
    h_here, w_here = hidden, weight
    ab = pl.pallas_call(
        functools.partial(update_kernel, group[0]),
        out_shape=jax.ShapeDtypeStruct((rows_a + rows_b, rank), bf16),
        in_specs=[vmem] * 4,
        out_specs=vmem,
        compiler_params=params,
        cost_estimate=cost(U_FLOPS, 8 * rank * rows_a),
        name="update",
    )(old, mine, other_a, other_b)
    ab_far = send(ab, group, Z2, name="ab_far")
    w1, _ = lax.optimization_barrier((w1, ab))
    w3 = send(w1, group, X, name="w3")
    w4 = send(w1, group, Y, name="w4")
    w5 = send(w1, group, Z1, Z2, name="w5")
    ab_0 = jnp.concatenate([ab, ab_far])
    ab_1 = send(ab_0, group, Z1, name="ab_1")
    ab_2 = send(ab_0, group, Y, name="ab_2")
    w3, w4, w5 = lax.optimization_barrier((w3, w4, w5))
    w6 = send(w4, group, X, name="w6")
    w7 = send(w4, group, Z1, Z2, name="w7")
    ab_3 = send(ab_1, group, Y, name="ab_3")
    held = [w0, w1, w2, w3, w4, w5, w6, w7]
    other_0 = send(ab_0, group, CORE, name="other_0")
    other_1 = send(ab_1, group, CORE, name="other_1")
    other_2 = send(ab_2, group, CORE, name="other_2")
    other_3 = send(ab_3, group, CORE, name="other_3")
    held, other_0, other_1, other_2 = lax.optimization_barrier((held, other_0, other_1, other_2))

    columns = outputs // 2
    held[0] = w_here
    own, other = pl.pallas_call(
        weight_kernel,
        out_shape=[jax.ShapeDtypeStruct((tokens, columns), f32)] * 2,
        in_specs=[vmem] * (2 + len(held)),
        out_specs=[vmem] * 2,
        scratch_shapes=[pltpu.VMEM((columns, depth), bf16)],
        compiler_params=params,
        cost_estimate=cost(W_FLOPS * 2 * tokens * outputs * depth, 2 * depth * (2 * tokens + columns)),
        name="weight_product",
    )(h_here, other_hidden, *held)
    received = send(other, group, CORE, name="received")
    middle = (0, 1, 2)
    t, merged, b_all = pl.pallas_call(
        functools.partial(middle_kernel, middle),
        out_shape=[
            jax.ShapeDtypeStruct((tokens, rank), f32),
            jax.ShapeDtypeStruct(weight.shape, bf16),
            jax.ShapeDtypeStruct((outputs, rank), bf16),
        ],
        in_specs=[vmem] * (2 + 2 * len(middle)),
        out_specs=[vmem] * 3,
        compiler_params=params,
        cost_estimate=cost(M_FLOPS * 2 * tokens * rank * depth, 2 * depth * (tokens + rank)),
        name="middle",
    )(h_here, w_here, ab_0, ab_1, ab_2, other_0, other_1, other_2)
    return tuple(pl.pallas_call(
        functools.partial(last_kernel, (3,)),
        out_shape=[
            jax.ShapeDtypeStruct((tokens, outputs), bf16),
            jax.ShapeDtypeStruct(weight.shape, bf16),
        ],
        in_specs=[vmem] * 10,
        out_specs=[vmem] * 2,
        scratch_shapes=[pltpu.VMEM((outputs, rank), bf16)],
        compiler_params=params,
        cost_estimate=cost(2 * tokens * rank * outputs, 2 * outputs * tokens),
        name="last",
    )(h_here, w_here, own, received, t, merged, b_all, ab_0, ab_3, other_3))


def solution(mesh):
    paired_fits = mesh.shape["rep"] == 2 and mesh.shape["fsdp"] == 16
    return jax.shard_map(
        paired if paired_fits else general,
        mesh=mesh,
        in_specs=(
            P(("rep", "fsdp"), None),
            P("fsdp", None),
            P("fsdp", None),
            P("fsdp", None),
            P("rep", "fsdp", None),
            P("rep", "fsdp", None),
        ),
        out_specs=(P(("rep", "fsdp"), None), P("fsdp", None)),
        check_vma=False,
    )
```

```python
import functools

import jax
import jax.numpy as jnp
from jax import lax
from jax.experimental import pallas as pl
from jax.experimental.pallas import tpu as pltpu
from jax.sharding import PartitionSpec as P

step_size = 0.5
AXES = ("rep", "fsdp")
NT = (((1,), (1,)), ((), ()))
NN = (((1,), (0,)), ((), ()))
VMEM_LIMIT = 16 * 1024 * 1024
WIDE_LIMIT = 58 * 1024 * 1024
EARLY = 6
U_FLOPS = 4e9
L_FLOPS = 1e6
P_FLOPS = 0
W_FLOPS = 1
M_FLOPS = 1


def dot(a, b, dims):
    return lax.dot_general(a, b, dims, preferred_element_type=jnp.float32)


def general(hidden, weight, adapter_a, adapter_b, grad_a, grad_b):
    replicas = lax.axis_size("rep")
    summed = lax.psum((grad_a[0], grad_b[0]), "rep")
    new_a = adapter_a - step_size * (summed[0] / replicas)
    new_b = adapter_b - step_size * (summed[1] / replicas)
    full_a = lax.all_gather(new_a, "fsdp", axis=0, tiled=True)
    delta = lax.dot_general(new_b, full_a, NT, precision=lax.Precision.HIGHEST, preferred_element_type=jnp.float32)
    own_rows = (weight.astype(jnp.float32) + delta).astype(jnp.bfloat16)
    output = dot(hidden, lax.all_gather(own_rows, "fsdp", axis=0, tiled=True), NT)
    return output.astype(jnp.bfloat16), own_rows


CORE, Y, Z1, Z2 = (0, 1), (0, 2), (0, 4), (0, 8)
REPLICA, X = (1, 0), (1, 1)
ZY1, ZY2 = (0, 6), (0, 10)


def send(rows, group, move, other_move=None, name="sent"):
    reps, shards = group
    pairs = []
    for r in range(reps):
        for f in range(shards):
            dr, df = move if (f & 1) == r or other_move is None else other_move
            pairs.append((r * shards + f, (r ^ dr) * shards + (f ^ df)))
    with jax.named_scope(name):
        return lax.ppermute(rows, AXES, pairs)


HELD = (
    ((0, 0, 0), (0, 0, 1)),
    ((2, 0, 0), (1, 0, 1)),
    ((0, 1, 0), (0, 1, 1)),
    ((2, 0, 1), (1, 0, 0)),
    ((2, 1, 0), (1, 1, 1)),
    ((3, 0, 0), (3, 0, 1)),
    ((2, 1, 1), (1, 1, 0)),
    ((3, 1, 0), (3, 1, 1)),
)
SHARDS = (((0, 0), (2, 0)), ((1, 0), (3, 0)), ((0, 1), (2, 1)), ((1, 1), (3, 1)))


def position():
    x, f = lax.axis_index("rep"), lax.axis_index("fsdp")
    return x, f >> 1, f & 1


def flips_of(i, kind):
    first, second = HELD[i]
    return [a + kind * (b - a) for a, b in zip(first, second)]


def shard_of(flips):
    x, place, _ = position()
    return (place ^ (flips[0] * 2 + flips[1])) * 2 + (x ^ flips[2])


def update_kernel(replicas, old_ref, own_ref, oa_ref, ob_ref, ab_ref):
    rows_a = oa_ref.shape[1]
    ab_ref[:rows_a] = (old_ref[:rows_a] - step_size * ((own_ref[:rows_a] + oa_ref[0]) / replicas)).astype(jnp.bfloat16)
    ab_ref[rows_a:] = (old_ref[rows_a:] - step_size * ((own_ref[rows_a:] + ob_ref[0]) / replicas)).astype(jnp.bfloat16)


def weight_kernel(h_ref, hs_ref, *refs):
    *shard_refs, own_ref, other_ref, w_all = refs
    rows = shard_refs[0].shape[0]
    for i, ref in enumerate(shard_refs):
        w_all[i * rows : (i + 1) * rows] = ref[...]
    other_ref[...] = dot(hs_ref[...], w_all[...], NT)
    own_ref[...] = dot(h_ref[...], w_all[...], NT)


def place(block_of, rows, products, out):
    n, m = products.shape[1], out.shape[1]
    source = lax.broadcasted_iota(jnp.int32, (n, m), 0)
    target = lax.broadcasted_iota(jnp.int32, (n, m), 1)
    column = jnp.zeros((n, m), jnp.int32)
    for i, (held, kind) in enumerate(block_of):
        column = jnp.where(source // rows == i, shard_of(flips_of(held, kind)) * rows, column)
    columns = (target == column + source % rows).astype(jnp.bfloat16)
    for part in split_bf16(products):
        out = out + dot(part, columns, NN)
    return out


def split_bf16(v):
    high = v.astype(jnp.bfloat16)
    return high, (v - high.astype(jnp.float32)).astype(jnp.bfloat16)


def add_blocks(h_ref, w_ref, b_own, merged_ref, b_all, blocks, t):
    x, place, core = position()
    rows_b = w_ref.shape[0]
    rows_a = h_ref.shape[1] * rows_b // b_all.shape[0]
    for ref, other, at, first in blocks:
        for j, (dz, dy) in enumerate(SHARDS[at], first):
            shard = (place ^ (dz * 2 + dy)) * 2 + (core ^ other)
            row = j * (rows_a + rows_b)
            columns = pl.ds(pl.multiple_of(shard * rows_a, rows_a), rows_a)
            part = ref[row : row + rows_a]
            b_all[pl.ds(pl.multiple_of(shard * rows_b, rows_b), rows_b)] = ref[row + rows_a : row + rows_a + rows_b]
            t = t + dot(h_ref[:, columns], part, NN)
            merged_ref[:, columns] = (w_ref[:, columns].astype(jnp.float32) + dot(b_own, part, NT)).astype(jnp.bfloat16)
    return t


def middle_kernel(at, early, h_ref, w_ref, own_ref, received_ref, *refs):
    *ab_refs, t_ref, high_ref, merged_ref, b_all = refs
    x, place_at, core = position()
    kind = core ^ x
    rows_b = w_ref.shape[0]
    rows_a = h_ref.shape[1] * rows_b // b_all.shape[0]
    out = jnp.zeros(high_ref.shape, jnp.float32)
    for ref, which in ((own_ref, kind), (received_ref, 1 - kind)):
        out = place([(i, which) for i in range(early)], rows_b, ref[...], out)
    high_ref[...] = out
    b_own = ab_refs[0][rows_a : rows_a + rows_b]
    n = len(at)
    blocks = [(ref, 0, at[i], 0) for i, ref in enumerate(ab_refs[:n])]
    joined = len(ab_refs) == n + 1
    blocks += [(ab_refs[n if joined else n + i], 1, k, 2 * i if joined else 0) for i, k in enumerate(at)]
    t_ref[...] = add_blocks(h_ref, w_ref, b_own, merged_ref, b_all, blocks, jnp.zeros(t_ref.shape, jnp.float32))


def late_kernel(late, h_ref, high_ref, *refs):
    *w_refs, out_ref = refs
    x, _, core = position()
    kind = core ^ x
    held = [(i, which) for which in (kind, 1 - kind) for i in late]
    products = dot(h_ref[...], jnp.concatenate([ref[...] for ref in w_refs]), NT)
    out_ref[...] = place(held, w_refs[0].shape[0], products, high_ref[...])


def last_kernel(at, h_ref, w_ref, t_ref, high_ref, m_ref, b_ref, first_ref, *refs):
    *ab_refs, out_ref, merged_ref, b_all = refs
    rows_b = w_ref.shape[0]
    rows_a = h_ref.shape[1] * rows_b // b_all.shape[0]
    b_own = first_ref[rows_a : rows_a + rows_b]
    merged_ref[...] = m_ref[...]
    b_all[...] = b_ref[...]
    blocks = [(ref, i // len(at), at[i % len(at)], 0) for i, ref in enumerate(ab_refs)]
    t = add_blocks(h_ref, w_ref, b_own, merged_ref, b_all, blocks, t_ref[...])
    out = high_ref[...]
    for part in split_bf16(t):
        out = out + dot(part, b_all[...], NT)
    out_ref[...] = out.astype(jnp.bfloat16)


def pick_kernel(first_ref, second_ref, out_ref):
    x, _, core = position()

    @pl.when(core == x)
    def _():
        out_ref[...] = first_ref[...]

    @pl.when(core != x)
    def _():
        out_ref[...] = second_ref[...]


def cost(flops, number_of_bytes):
    return pl.CostEstimate(flops=int(flops), bytes_accessed=int(number_of_bytes), transcendentals=0)


def paired(hidden, weight, adapter_a, adapter_b, grad_a, grad_b):
    group = (lax.axis_size("rep"), lax.axis_size("fsdp"))
    tokens, depth = hidden.shape
    rank = adapter_a.shape[1]
    rows_a, rows_b = adapter_a.shape[0], weight.shape[0]
    outputs = rows_b * group[1]

    any_space = pl.BlockSpec(memory_space=pltpu.HBM)
    vmem = pl.BlockSpec(memory_space=pltpu.VMEM)
    params = pltpu.CompilerParams(vmem_limit_bytes=VMEM_LIMIT)
    wide = pltpu.CompilerParams(vmem_limit_bytes=WIDE_LIMIT)
    bf16, f32 = jnp.bfloat16, jnp.float32

    hold = lax.optimization_barrier
    h_here, w_here = hidden, weight
    old = jnp.concatenate([adapter_a, adapter_b])
    mine = jnp.concatenate([grad_a[0], grad_b[0]])
    old, mine = hold((old, mine))
    w0 = weight
    other_a = send(grad_a, group, REPLICA, name="other_a")
    other_b = send(grad_b, group, REPLICA, name="other_b")
    w1 = send(w0, group, Z2, Z1, name="w1")
    w2 = send(w0, group, Y, name="w2")
    w1, w2 = hold((w1, w2))
    other_hidden = send(hidden, group, CORE, name="other_hidden")
    ab = pl.pallas_call(
        functools.partial(update_kernel, group[0]),
        out_shape=jax.ShapeDtypeStruct((rows_a + rows_b, rank), bf16),
        in_specs=[vmem] * 4,
        out_specs=vmem,
        compiler_params=params,
        cost_estimate=cost(U_FLOPS, 8 * rank * rows_a),
        name="update",
    )(old, mine, other_a, other_b)
    ab_far = send(ab, group, Z2, name="ab_far")
    w3 = send(w1, group, X, name="w3")
    w4 = send(w1, group, Y, name="w4")
    w5 = send(w1, group, Z1, Z2, name="w5")
    ab_0 = jnp.concatenate([ab, ab_far])
    ab_1 = send(ab_0, group, Z1, name="ab_1")
    ab_2 = send(ab_0, group, Y, name="ab_2")
    other_0 = send(ab_0, group, CORE, name="other_0")
    ab_3 = send(ab_1, group, Y, name="ab_3")
    w3, w4, w5 = hold((w3, w4, w5))
    w6 = send(w4, group, X, name="w6")
    mixed = pl.pallas_call(
        pick_kernel,
        out_shape=jax.ShapeDtypeStruct(weight.shape, bf16),
        in_specs=[vmem] * 2,
        out_specs=vmem,
        compiler_params=params,
        cost_estimate=cost(P_FLOPS, 0),
        name="pick",
    )(w4, w5)
    w7 = send(mixed, group, Z1, Y, name="w7")
    held = [w0, w1, w2, w3, w4, w5, w6, w7]
    other_1 = send(ab_1, group, CORE, name="other_1")
    other_2 = send(ab_2, group, CORE, name="other_2")
    other_3 = send(ab_3, group, CORE, name="other_3")
    ab_early = [ab_0, ab_1, ab_2, other_0, other_1, other_2]

    early = [w_here] + held[1:EARLY]
    late = held[EARLY:]
    early, other_0 = lax.optimization_barrier((early, other_0))
    ab_early = [ab_0, ab_1, ab_2, other_0, other_1, other_2]
    columns = rows_b * EARLY
    own, other = pl.pallas_call(
        weight_kernel,
        out_shape=[jax.ShapeDtypeStruct((tokens, columns), f32)] * 2,
        in_specs=[vmem] * (2 + EARLY),
        out_specs=[vmem] * 2,
        scratch_shapes=[pltpu.VMEM((columns, depth), bf16)],
        compiler_params=params,
        cost_estimate=cost(W_FLOPS * 4 * tokens * columns * depth, 2 * depth * (2 * tokens + columns)),
        name="weight_product",
    )(h_here, other_hidden, *early)
    received = send(other, group, CORE, name="received")
    middle = (0, 1, 2)
    t, high, merged, b_all = pl.pallas_call(
        functools.partial(middle_kernel, middle, EARLY),
        out_shape=[
            jax.ShapeDtypeStruct((tokens, rank), f32),
            jax.ShapeDtypeStruct((tokens, outputs), f32),
            jax.ShapeDtypeStruct(weight.shape, bf16),
            jax.ShapeDtypeStruct((outputs, rank), bf16),
        ],
        in_specs=[vmem] * (4 + len(ab_early)),
        out_specs=[vmem] * 4,
        compiler_params=params,
        cost_estimate=cost(M_FLOPS * 2 * tokens * rank * depth, 2 * depth * (tokens + rank)),
        name="middle",
    )(h_here, w_here, own, received, *ab_early)
    late, t = lax.optimization_barrier((late, t))
    other_late = [send(v, group, CORE, name="other_late") for v in late]
    high = pl.pallas_call(
        functools.partial(late_kernel, tuple(range(EARLY, len(HELD)))),
        out_shape=jax.ShapeDtypeStruct((tokens, outputs), f32),
        in_specs=[vmem] * (2 + 2 * len(late)),
        out_specs=vmem,
        compiler_params=params,
        cost_estimate=cost(L_FLOPS, 2 * outputs * tokens),
        name="late_product",
    )(h_here, high, *late, *other_late)
    return tuple(pl.pallas_call(
        functools.partial(last_kernel, (3,)),
        out_shape=[
            jax.ShapeDtypeStruct((tokens, outputs), bf16),
            jax.ShapeDtypeStruct(weight.shape, bf16),
        ],
        in_specs=[vmem] * 9,
        out_specs=[vmem] * 2,
        scratch_shapes=[pltpu.VMEM((outputs, rank), bf16)],
        compiler_params=params,
        cost_estimate=cost(2 * tokens * rank * outputs, 2 * outputs * tokens),
        name="last",
    )(h_here, w_here, t, high, merged, b_all, ab_0, ab_3, other_3))


def solution(mesh):
    paired_fits = mesh.shape["rep"] == 2 and mesh.shape["fsdp"] == 16
    return jax.shard_map(
        paired if paired_fits else general,
        mesh=mesh,
        in_specs=(
            P(("rep", "fsdp"), None),
            P("fsdp", None),
            P("fsdp", None),
            P("fsdp", None),
            P("rep", "fsdp", None),
            P("rep", "fsdp", None),
        ),
        out_specs=(P(("rep", "fsdp"), None), P("fsdp", None)),
        check_vma=False,
    )
```

```python
import functools

import jax
import jax.numpy as jnp
from jax import lax
from jax.experimental import pallas as pl
from jax.experimental.pallas import tpu as pltpu
from jax.sharding import PartitionSpec as P

step_size = 0.5
AXES = ("rep", "fsdp")
NT = (((1,), (1,)), ((), ()))
NN = (((1,), (0,)), ((), ()))
VMEM_LIMIT = 16 * 1024 * 1024
EARLY = 6
U_FLOPS = 4e9
L_FLOPS = 1e6
W_FLOPS = 4
M_FLOPS = 1


def dot(a, b, dims):
    return lax.dot_general(a, b, dims, preferred_element_type=jnp.float32)


def general(hidden, weight, adapter_a, adapter_b, grad_a, grad_b):
    replicas = lax.axis_size("rep")
    summed = lax.psum((grad_a[0], grad_b[0]), "rep")
    new_a = adapter_a - step_size * (summed[0] / replicas)
    new_b = adapter_b - step_size * (summed[1] / replicas)
    full_a = lax.all_gather(new_a, "fsdp", axis=0, tiled=True)
    delta = lax.dot_general(new_b, full_a, NT, precision=lax.Precision.HIGHEST, preferred_element_type=jnp.float32)
    own_rows = (weight.astype(jnp.float32) + delta).astype(jnp.bfloat16)
    output = dot(hidden, lax.all_gather(own_rows, "fsdp", axis=0, tiled=True), NT)
    return output.astype(jnp.bfloat16), own_rows


CORE, Y, Z1, Z2 = (0, 1), (0, 2), (0, 4), (0, 8)
REPLICA, X = (1, 0), (1, 1)


def send(rows, group, move, other_move=None, name="sent"):
    reps, shards = group
    pairs = []
    for r in range(reps):
        for f in range(shards):
            dr, df = move if (f & 1) == r or other_move is None else other_move
            pairs.append((r * shards + f, (r ^ dr) * shards + (f ^ df)))
    with jax.named_scope(name):
        return lax.ppermute(rows, AXES, pairs)


HELD = (
    ((0, 0, 0), (0, 0, 1)),
    ((2, 0, 0), (1, 0, 1)),
    ((0, 1, 0), (0, 1, 1)),
    ((2, 0, 1), (1, 0, 0)),
    ((2, 1, 0), (1, 1, 1)),
    ((3, 0, 0), (3, 0, 1)),
    ((2, 1, 1), (1, 1, 0)),
    ((3, 1, 0), (3, 1, 1)),
)
SHARDS = (((0, 0), (2, 0)), ((1, 0), (3, 0)), ((0, 1), (2, 1)), ((1, 1), (3, 1)))


def position():
    x, f = lax.axis_index("rep"), lax.axis_index("fsdp")
    return x, f >> 1, f & 1


def flips_of(i, kind):
    first, second = HELD[i]
    return [a + kind * (b - a) for a, b in zip(first, second)]


def shard_of(flips):
    x, place, _ = position()
    return (place ^ (flips[0] * 2 + flips[1])) * 2 + (x ^ flips[2])


def update_kernel(replicas, old_ref, own_ref, oa_ref, ob_ref, ab_ref):
    rows_a = oa_ref.shape[1]
    ab_ref[:rows_a] = (old_ref[:rows_a] - step_size * ((own_ref[:rows_a] + oa_ref[0]) / replicas)).astype(jnp.bfloat16)
    ab_ref[rows_a:] = (old_ref[rows_a:] - step_size * ((own_ref[rows_a:] + ob_ref[0]) / replicas)).astype(jnp.bfloat16)


def weight_kernel(h_ref, hs_ref, *refs):
    *shard_refs, own_ref, other_ref, w_all = refs
    rows = shard_refs[0].shape[0]
    for i, ref in enumerate(shard_refs):
        w_all[i * rows : (i + 1) * rows] = ref[...]
    other_ref[...] = dot(hs_ref[...], w_all[...], NT)
    own_ref[...] = dot(h_ref[...], w_all[...], NT)


def place(block_of, rows, products, out):
    n, m = products.shape[1], out.shape[1]
    source = lax.broadcasted_iota(jnp.int32, (n, m), 0)
    target = lax.broadcasted_iota(jnp.int32, (n, m), 1)
    column = jnp.zeros((n, m), jnp.int32)
    for i, (held, kind) in enumerate(block_of):
        column = jnp.where(source // rows == i, shard_of(flips_of(held, kind)) * rows, column)
    columns = (target == column + source % rows).astype(jnp.bfloat16)
    for part in split_bf16(products):
        out = out + dot(part, columns, NN)
    return out


def split_bf16(v):
    high = v.astype(jnp.bfloat16)
    return high, (v - high.astype(jnp.float32)).astype(jnp.bfloat16)


def add_blocks(h_ref, w_ref, b_own, merged_ref, b_all, blocks, t):
    x, place, core = position()
    rows_b = w_ref.shape[0]
    rows_a = h_ref.shape[1] * rows_b // b_all.shape[0]
    for ref, other, at, first in blocks:
        for j, (dz, dy) in enumerate(SHARDS[at], first):
            shard = (place ^ (dz * 2 + dy)) * 2 + (core ^ other)
            row = j * (rows_a + rows_b)
            columns = pl.ds(pl.multiple_of(shard * rows_a, rows_a), rows_a)
            part = ref[row : row + rows_a]
            b_all[pl.ds(pl.multiple_of(shard * rows_b, rows_b), rows_b)] = ref[row + rows_a : row + rows_a + rows_b]
            t = t + dot(h_ref[:, columns], part, NN)
            merged_ref[:, columns] = (w_ref[:, columns].astype(jnp.float32) + dot(b_own, part, NT)).astype(jnp.bfloat16)
    return t


def middle_kernel(at, early, h_ref, w_ref, own_ref, received_ref, *refs):
    *ab_refs, t_ref, high_ref, merged_ref, b_all = refs
    x, place_at, core = position()
    kind = core ^ x
    rows_b = w_ref.shape[0]
    rows_a = h_ref.shape[1] * rows_b // b_all.shape[0]
    out = jnp.zeros(high_ref.shape, jnp.float32)
    for ref, which in ((own_ref, kind), (received_ref, 1 - kind)):
        out = place([(i, which) for i in range(early)], rows_b, ref[...], out)
    high_ref[...] = out
    b_own = ab_refs[0][rows_a : rows_a + rows_b]
    n = len(at)
    blocks = [(ref, 0, at[i], 0) for i, ref in enumerate(ab_refs[:n])]
    rest = ab_refs[n:]
    separate = len(rest) if len(rest) == n else len(rest) - 1
    blocks += [(rest[i], 1, at[i], 0) for i in range(separate)]
    blocks += [(rest[-1], 1, at[i], 2 * (i - separate)) for i in range(separate, n)]
    t_ref[...] = add_blocks(h_ref, w_ref, b_own, merged_ref, b_all, blocks, jnp.zeros(t_ref.shape, jnp.float32))


def late_kernel(late, h_ref, high_ref, *refs):
    *w_refs, out_ref = refs
    x, _, core = position()
    kind = core ^ x
    held = [(i, which) for which in (kind, 1 - kind) for i in late]
    products = dot(h_ref[...], jnp.concatenate([ref[...] for ref in w_refs]), NT)
    out_ref[...] = place(held, w_refs[0].shape[0], products, high_ref[...])


def last_kernel(at, h_ref, w_ref, t_ref, high_ref, m_ref, b_ref, first_ref, *refs):
    *ab_refs, out_ref, merged_ref, b_all = refs
    rows_b = w_ref.shape[0]
    rows_a = h_ref.shape[1] * rows_b // b_all.shape[0]
    b_own = first_ref[rows_a : rows_a + rows_b]
    merged_ref[...] = m_ref[...]
    b_all[...] = b_ref[...]
    blocks = [(ref, i // len(at), at[i % len(at)], 0) for i, ref in enumerate(ab_refs)]
    t = add_blocks(h_ref, w_ref, b_own, merged_ref, b_all, blocks, t_ref[...])
    out = high_ref[...]
    for part in split_bf16(t):
        out = out + dot(part, b_all[...], NT)
    out_ref[...] = out.astype(jnp.bfloat16)


def cost(flops, number_of_bytes):
    return pl.CostEstimate(flops=int(flops), bytes_accessed=int(number_of_bytes), transcendentals=0)


def paired(hidden, weight, adapter_a, adapter_b, grad_a, grad_b):
    group = (lax.axis_size("rep"), lax.axis_size("fsdp"))
    tokens, depth = hidden.shape
    rank = adapter_a.shape[1]
    rows_a, rows_b = adapter_a.shape[0], weight.shape[0]
    outputs = rows_b * group[1]

    vmem = pl.BlockSpec(memory_space=pltpu.VMEM)
    params = pltpu.CompilerParams(vmem_limit_bytes=VMEM_LIMIT)
    bf16, f32 = jnp.bfloat16, jnp.float32

    hold = lax.optimization_barrier
    h_here, w_here = hidden, weight
    old = jnp.concatenate([adapter_a, adapter_b])
    mine = jnp.concatenate([grad_a[0], grad_b[0]])
    old, mine = hold((old, mine))
    w0 = weight
    other_a = send(grad_a, group, REPLICA, name="other_a")
    other_b = send(grad_b, group, REPLICA, name="other_b")
    w1 = send(w0, group, Z2, Z1, name="w1")
    w2 = send(w0, group, Y, name="w2")
    w1, w2 = hold((w1, w2))
    other_hidden = send(hidden, group, CORE, name="other_hidden")
    ab = pl.pallas_call(
        functools.partial(update_kernel, group[0]),
        out_shape=jax.ShapeDtypeStruct((rows_a + rows_b, rank), bf16),
        in_specs=[vmem] * 4,
        out_specs=vmem,
        compiler_params=params,
        cost_estimate=cost(U_FLOPS, 8 * rank * rows_a),
        name="update",
    )(old, mine, other_a, other_b)
    ab_far = send(ab, group, Z2, name="ab_far")
    w3 = send(w1, group, X, name="w3")
    w4 = send(w1, group, Y, name="w4")
    w5 = send(w1, group, Z1, Z2, name="w5")
    ab_0 = jnp.concatenate([ab, ab_far])
    ab_1 = send(ab_0, group, Z1, name="ab_1")
    ab_2 = send(ab_0, group, Y, name="ab_2")
    other_0 = send(ab_0, group, CORE, name="other_0")
    ab_3 = send(ab_2, group, Z1, name="ab_3")
    w3, w4 = hold((w3, w4))
    w6 = send(w4, group, X, name="w6")
    w7 = send(w5, group, Y, name="w7")
    held = [w0, w1, w2, w3, w4, w5, w6, w7]
    other_1 = send(ab_1, group, CORE, name="other_1")
    other_2 = send(ab_2, group, CORE, name="other_2")
    other_3 = send(ab_3, group, CORE, name="other_3")
    ab_early = [ab_0, ab_1, ab_2, other_0, other_1, other_2]

    early = [w_here] + held[1:EARLY]
    late = held[EARLY:]
    early, other_0 = lax.optimization_barrier((early, other_0))
    ab_early = [ab_0, ab_1, ab_2, other_0, other_1, other_2]
    columns = rows_b * EARLY
    own, other = pl.pallas_call(
        weight_kernel,
        out_shape=[jax.ShapeDtypeStruct((tokens, columns), f32)] * 2,
        in_specs=[vmem] * (2 + EARLY),
        out_specs=[vmem] * 2,
        scratch_shapes=[pltpu.VMEM((columns, depth), bf16)],
        compiler_params=params,
        cost_estimate=cost(W_FLOPS * 4 * tokens * columns * depth, 2 * depth * (2 * tokens + columns)),
        name="weight_product",
    )(h_here, other_hidden, *early)
    received = send(other, group, CORE, name="received")
    middle = (0, 1, 2)
    t, high, merged, b_all = pl.pallas_call(
        functools.partial(middle_kernel, middle, EARLY),
        out_shape=[
            jax.ShapeDtypeStruct((tokens, rank), f32),
            jax.ShapeDtypeStruct((tokens, outputs), f32),
            jax.ShapeDtypeStruct(weight.shape, bf16),
            jax.ShapeDtypeStruct((outputs, rank), bf16),
        ],
        in_specs=[vmem] * (4 + len(ab_early)),
        out_specs=[vmem] * 4,
        compiler_params=params,
        cost_estimate=cost(M_FLOPS * 2 * tokens * rank * depth, 2 * depth * (tokens + rank)),
        name="middle",
    )(h_here, w_here, own, received, *ab_early)
    late, t = lax.optimization_barrier((late, t))
    other_late = [send(v, group, CORE, name="other_late") for v in late]
    high = pl.pallas_call(
        functools.partial(late_kernel, tuple(range(EARLY, len(HELD)))),
        out_shape=jax.ShapeDtypeStruct((tokens, outputs), f32),
        in_specs=[vmem] * (2 + 2 * len(late)),
        out_specs=vmem,
        compiler_params=params,
        cost_estimate=cost(L_FLOPS, 2 * outputs * tokens),
        name="late_product",
    )(h_here, high, *late, *other_late)
    return tuple(pl.pallas_call(
        functools.partial(last_kernel, (3,)),
        out_shape=[
            jax.ShapeDtypeStruct((tokens, outputs), bf16),
            jax.ShapeDtypeStruct(weight.shape, bf16),
        ],
        in_specs=[vmem] * 9,
        out_specs=[vmem] * 2,
        scratch_shapes=[pltpu.VMEM((outputs, rank), bf16)],
        compiler_params=params,
        cost_estimate=cost(2 * tokens * rank * outputs, 2 * outputs * tokens),
        name="last",
    )(h_here, w_here, t, high, merged, b_all, ab_0, ab_3, other_3))


def solution(mesh):
    paired_fits = mesh.shape["rep"] == 2 and mesh.shape["fsdp"] == 16
    return jax.shard_map(
        paired if paired_fits else general,
        mesh=mesh,
        in_specs=(
            P(("rep", "fsdp"), None),
            P("fsdp", None),
            P("fsdp", None),
            P("fsdp", None),
            P("rep", "fsdp", None),
            P("rep", "fsdp", None),
        ),
        out_specs=(P(("rep", "fsdp"), None), P("fsdp", None)),
        check_vma=False,
    )
```

```python
import functools

import jax
import jax.numpy as jnp
from jax import lax
from jax.experimental import pallas as pl
from jax.experimental.pallas import tpu as pltpu
from jax.sharding import PartitionSpec as P

step_size = 0.5
AXES = ("rep", "fsdp")
NT = (((1,), (1,)), ((), ()))
NN = (((1,), (0,)), ((), ()))
VMEM_LIMIT = 8 * 1024 * 1024
EARLY = 6
U_FLOPS = 4e9
L_FLOPS = 1e9
W_FLOPS = 4
M_FLOPS = 1


def dot(a, b, dims):
    return lax.dot_general(a, b, dims, preferred_element_type=jnp.float32)


def general(hidden, weight, adapter_a, adapter_b, grad_a, grad_b):
    replicas = lax.axis_size("rep")
    summed = lax.psum((grad_a[0], grad_b[0]), "rep")
    new_a = adapter_a - step_size * (summed[0] / replicas)
    new_b = adapter_b - step_size * (summed[1] / replicas)
    full_a = lax.all_gather(new_a, "fsdp", axis=0, tiled=True)
    delta = lax.dot_general(new_b, full_a, NT, precision=lax.Precision.HIGHEST, preferred_element_type=jnp.float32)
    own_rows = (weight.astype(jnp.float32) + delta).astype(jnp.bfloat16)
    output = dot(hidden, lax.all_gather(own_rows, "fsdp", axis=0, tiled=True), NT)
    return output.astype(jnp.bfloat16), own_rows


CORE, Y, Z1, Z2 = (0, 1), (0, 2), (0, 4), (0, 8)
REPLICA, X = (1, 0), (1, 1)


def send(rows, group, move, other_move=None, name="sent"):
    reps, shards = group
    pairs = []
    for r in range(reps):
        for f in range(shards):
            dr, df = move if (f & 1) == r or other_move is None else other_move
            pairs.append((r * shards + f, (r ^ dr) * shards + (f ^ df)))
    with jax.named_scope(name):
        return lax.ppermute(rows, AXES, pairs)


HELD = (
    ((0, 0, 0), (0, 0, 1)),
    ((2, 0, 0), (1, 0, 1)),
    ((0, 1, 0), (0, 1, 1)),
    ((2, 0, 1), (1, 0, 0)),
    ((2, 1, 0), (1, 1, 1)),
    ((3, 0, 0), (3, 0, 1)),
    ((2, 1, 1), (1, 1, 0)),
    ((3, 1, 0), (3, 1, 1)),
)
SHARDS = (((0, 0), (2, 0)), ((1, 0), (3, 0)), ((0, 1), (2, 1)), ((1, 1), (3, 1)))


def position():
    x, f = lax.axis_index("rep"), lax.axis_index("fsdp")
    return x, f >> 1, f & 1


def flips_of(i, kind):
    first, second = HELD[i]
    return [a + kind * (b - a) for a, b in zip(first, second)]


def shard_of(flips):
    x, place, _ = position()
    return (place ^ (flips[0] * 2 + flips[1])) * 2 + (x ^ flips[2])


def update_kernel(replicas, old_ref, own_ref, oa_ref, ob_ref, ab_ref):
    rows_a = oa_ref.shape[1]
    ab_ref[:rows_a] = (old_ref[:rows_a] - step_size * ((own_ref[:rows_a] + oa_ref[0]) / replicas)).astype(jnp.bfloat16)
    ab_ref[rows_a:] = (old_ref[rows_a:] - step_size * ((own_ref[rows_a:] + ob_ref[0]) / replicas)).astype(jnp.bfloat16)


def weight_kernel(h_ref, hs_ref, *refs):
    *shard_refs, own_ref, other_ref, w_all = refs
    rows = shard_refs[0].shape[0]
    for i, ref in enumerate(shard_refs):
        w_all[i * rows : (i + 1) * rows] = ref[...]
    other_ref[...] = dot(hs_ref[...], w_all[...], NT)
    own_ref[...] = dot(h_ref[...], w_all[...], NT)


def place(block_of, rows, products, out):
    n, m = products.shape[1], out.shape[1]
    source = lax.broadcasted_iota(jnp.int32, (n, m), 0)
    target = lax.broadcasted_iota(jnp.int32, (n, m), 1)
    column = jnp.zeros((n, m), jnp.int32)
    for i, (held, kind) in enumerate(block_of):
        column = jnp.where(source // rows == i, shard_of(flips_of(held, kind)) * rows, column)
    columns = (target == column + source % rows).astype(jnp.bfloat16)
    for part in split_bf16(products):
        out = out + dot(part, columns, NN)
    return out


def split_bf16(v):
    high = v.astype(jnp.bfloat16)
    return high, (v - high.astype(jnp.float32)).astype(jnp.bfloat16)


def add_blocks(h_ref, w_ref, b_own, merged_ref, b_all, blocks, t):
    x, place, core = position()
    rows_b = w_ref.shape[0]
    rows_a = h_ref.shape[1] * rows_b // b_all.shape[0]
    for ref, other, at, first in blocks:
        for j, (dz, dy) in enumerate(SHARDS[at], first):
            shard = (place ^ (dz * 2 + dy)) * 2 + (core ^ other)
            row = j * (rows_a + rows_b)
            columns = pl.ds(pl.multiple_of(shard * rows_a, rows_a), rows_a)
            part = ref[row : row + rows_a]
            b_all[pl.ds(pl.multiple_of(shard * rows_b, rows_b), rows_b)] = ref[row + rows_a : row + rows_a + rows_b]
            t = t + dot(h_ref[:, columns], part, NN)
            merged_ref[:, columns] = (w_ref[:, columns].astype(jnp.float32) + dot(b_own, part, NT)).astype(jnp.bfloat16)
    return t


def middle_kernel(at, others, early, h_ref, w_ref, own_ref, received_ref, *refs):
    *ab_refs, t_ref, high_ref, merged_ref, b_all = refs
    x, place_at, core = position()
    kind = core ^ x
    rows_b = w_ref.shape[0]
    rows_a = h_ref.shape[1] * rows_b // b_all.shape[0]
    out = jnp.zeros(high_ref.shape, jnp.float32)
    for ref, which in ((own_ref, kind), (received_ref, 1 - kind)):
        out = place([(i, which) for i in range(early)], rows_b, ref[...], out)
    high_ref[...] = out
    b_own = ab_refs[0][rows_a : rows_a + rows_b]
    n = len(at)
    blocks = [(ref, 0, at[i], 0) for i, ref in enumerate(ab_refs[:n])]
    blocks += [(ref, 1, k, 0) for ref, k in zip(ab_refs[n:], others)]
    t_ref[...] = add_blocks(h_ref, w_ref, b_own, merged_ref, b_all, blocks, jnp.zeros(t_ref.shape, jnp.float32))


def late_kernel(late, h_ref, high_ref, *refs):
    *w_refs, out_ref = refs
    x, _, core = position()
    kind = core ^ x
    held = [(i, which) for which in (kind, 1 - kind) for i in late]
    products = dot(h_ref[...], jnp.concatenate([ref[...] for ref in w_refs]), NT)
    out_ref[...] = place(held, w_refs[0].shape[0], products, high_ref[...])


def last_kernel(at, h_ref, w_ref, t_ref, high_ref, m_ref, b_ref, first_ref, *refs):
    *ab_refs, out_ref, merged_ref, b_all = refs
    rows_b = w_ref.shape[0]
    rows_a = h_ref.shape[1] * rows_b // b_all.shape[0]
    b_own = first_ref[rows_a : rows_a + rows_b]
    merged_ref[...] = m_ref[...]
    b_all[...] = b_ref[...]
    own, joined = ab_refs
    blocks = [(own, 0, at[-1], 0)] + [(joined, 1, k, 2 * i) for i, k in enumerate(at)]
    t = add_blocks(h_ref, w_ref, b_own, merged_ref, b_all, blocks, t_ref[...])
    out = high_ref[...]
    for part in split_bf16(t):
        out = out + dot(part, b_all[...], NT)
    out_ref[...] = out.astype(jnp.bfloat16)


def cost(flops, number_of_bytes):
    return pl.CostEstimate(flops=int(flops), bytes_accessed=int(number_of_bytes), transcendentals=0)


def paired(hidden, weight, adapter_a, adapter_b, grad_a, grad_b):
    group = (lax.axis_size("rep"), lax.axis_size("fsdp"))
    tokens, depth = hidden.shape
    rank = adapter_a.shape[1]
    rows_a, rows_b = adapter_a.shape[0], weight.shape[0]
    outputs = rows_b * group[1]

    vmem = pl.BlockSpec(memory_space=pltpu.VMEM)
    params = pltpu.CompilerParams(vmem_limit_bytes=VMEM_LIMIT)
    bf16, f32 = jnp.bfloat16, jnp.float32

    hold = lax.optimization_barrier
    h_here, w_here = hidden, weight
    old = jnp.concatenate([adapter_a, adapter_b])
    mine = jnp.concatenate([grad_a[0], grad_b[0]])
    old, mine = hold((old, mine))
    w0 = weight
    other_a = send(grad_a, group, REPLICA, name="other_a")
    other_b = send(grad_b, group, REPLICA, name="other_b")
    w1 = send(w0, group, Z2, Z1, name="w1")
    w2 = send(w0, group, Y, name="w2")
    w1, w2 = hold((w1, w2))
    other_hidden = send(hidden, group, CORE, name="other_hidden")
    ab = pl.pallas_call(
        functools.partial(update_kernel, group[0]),
        out_shape=jax.ShapeDtypeStruct((rows_a + rows_b, rank), bf16),
        in_specs=[vmem] * 4,
        out_specs=vmem,
        compiler_params=params,
        cost_estimate=cost(U_FLOPS, 8 * rank * rows_a),
        name="update",
    )(old, mine, other_a, other_b)
    ab_far = send(ab, group, Z2, name="ab_far")
    w3 = send(w1, group, X, name="w3")
    w4 = send(w1, group, Y, name="w4")
    w5 = send(w1, group, Z1, Z2, name="w5")
    ab_0 = jnp.concatenate([ab, ab_far])
    ab_1 = send(ab_0, group, Z1, name="ab_1")
    ab_2 = send(ab_0, group, Y, name="ab_2")
    other_0 = send(ab_0, group, CORE, name="other_0")
    ab_3 = send(ab_2, group, Z1, name="ab_3")
    w3, w4 = hold((w3, w4))
    w6 = send(w4, group, X, name="w6")
    w7 = send(w5, group, Y, name="w7")
    held = [w0, w1, w2, w3, w4, w5, w6, w7]
    other_2 = send(ab_2, group, CORE, name="other_2")
    joined = jnp.concatenate([ab_1, ab_3])
    other_3 = send(joined, group, CORE, name="other_3")
    ab_early = [ab_0, ab_1, ab_2, other_0, other_2]

    early = [w_here] + held[1:EARLY]
    late = held[EARLY:]
    early, other_0 = lax.optimization_barrier((early, other_0))
    ab_early = [ab_0, ab_1, ab_2, other_0, other_2]
    columns = rows_b * EARLY
    own, other = pl.pallas_call(
        weight_kernel,
        out_shape=[jax.ShapeDtypeStruct((tokens, columns), f32)] * 2,
        in_specs=[vmem] * (2 + EARLY),
        out_specs=[vmem] * 2,
        scratch_shapes=[pltpu.VMEM((columns, depth), bf16)],
        compiler_params=params,
        cost_estimate=cost(W_FLOPS * 4 * tokens * columns * depth, 2 * depth * (2 * tokens + columns)),
        name="weight_product",
    )(h_here, other_hidden, *early)
    received = send(other, group, CORE, name="received")
    middle = (0, 1, 2)
    t, high, merged, b_all = pl.pallas_call(
        functools.partial(middle_kernel, middle, (0, 2), EARLY),
        out_shape=[
            jax.ShapeDtypeStruct((tokens, rank), f32),
            jax.ShapeDtypeStruct((tokens, outputs), f32),
            jax.ShapeDtypeStruct(weight.shape, bf16),
            jax.ShapeDtypeStruct((outputs, rank), bf16),
        ],
        in_specs=[vmem] * (4 + len(ab_early)),
        out_specs=[vmem] * 4,
        compiler_params=params,
        cost_estimate=cost(M_FLOPS * 2 * tokens * rank * depth, 2 * depth * (tokens + rank)),
        name="middle",
    )(h_here, w_here, own, received, *ab_early)
    late, t = lax.optimization_barrier((late, t))
    other_late = [send(v, group, CORE, name="other_late") for v in late]
    high = pl.pallas_call(
        functools.partial(late_kernel, tuple(range(EARLY, len(HELD)))),
        out_shape=jax.ShapeDtypeStruct((tokens, outputs), f32),
        in_specs=[vmem] * (2 + 2 * len(late)),
        out_specs=vmem,
        compiler_params=params,
        cost_estimate=cost(L_FLOPS, 2 * outputs * tokens),
        name="late_product",
    )(h_here, high, *late, *other_late)
    return tuple(pl.pallas_call(
        functools.partial(last_kernel, (1, 3)),
        out_shape=[
            jax.ShapeDtypeStruct((tokens, outputs), bf16),
            jax.ShapeDtypeStruct(weight.shape, bf16),
        ],
        in_specs=[vmem] * 9,
        out_specs=[vmem] * 2,
        scratch_shapes=[pltpu.VMEM((outputs, rank), bf16)],
        compiler_params=params,
        cost_estimate=cost(2 * tokens * rank * outputs, 2 * outputs * tokens),
        name="last",
    )(h_here, w_here, t, high, merged, b_all, ab_0, ab_3, other_3))


def solution(mesh):
    paired_fits = mesh.shape["rep"] == 2 and mesh.shape["fsdp"] == 16
    return jax.shard_map(
        paired if paired_fits else general,
        mesh=mesh,
        in_specs=(
            P(("rep", "fsdp"), None),
            P("fsdp", None),
            P("fsdp", None),
            P("fsdp", None),
            P("rep", "fsdp", None),
            P("rep", "fsdp", None),
        ),
        out_specs=(P(("rep", "fsdp"), None), P("fsdp", None)),
        check_vma=False,
    )
```

```python
import functools

import jax
import jax.numpy as jnp
from jax import lax
from jax.experimental import pallas as pl
from jax.experimental.pallas import tpu as pltpu
from jax.sharding import PartitionSpec as P

step_size = 0.5
AXES = ("rep", "fsdp")
NT = (((1,), (1,)), ((), ()))
NN = (((1,), (0,)), ((), ()))
VMEM_LIMIT = 8 * 1024 * 1024
EARLY = 6
U_FLOPS = 4e9
L_FLOPS = 1e9
W_FLOPS = 4
M_FLOPS = 1


def dot(a, b, dims):
    return lax.dot_general(a, b, dims, preferred_element_type=jnp.float32)


def general(hidden, weight, adapter_a, adapter_b, grad_a, grad_b):
    replicas = lax.axis_size("rep")
    summed = lax.psum((grad_a[0], grad_b[0]), "rep")
    new_a = adapter_a - step_size * (summed[0] / replicas)
    new_b = adapter_b - step_size * (summed[1] / replicas)
    full_a = lax.all_gather(new_a, "fsdp", axis=0, tiled=True)
    delta = lax.dot_general(new_b, full_a, NT, precision=lax.Precision.HIGHEST, preferred_element_type=jnp.float32)
    own_rows = (weight.astype(jnp.float32) + delta).astype(jnp.bfloat16)
    output = dot(hidden, lax.all_gather(own_rows, "fsdp", axis=0, tiled=True), NT)
    return output.astype(jnp.bfloat16), own_rows


CORE, Y, Z1, Z2 = (0, 1), (0, 2), (0, 4), (0, 8)
REPLICA, X = (1, 0), (1, 1)


def send(rows, group, move, other_move=None, name="sent"):
    reps, shards = group
    pairs = []
    for r in range(reps):
        for f in range(shards):
            dr, df = move if (f & 1) == r or other_move is None else other_move
            pairs.append((r * shards + f, (r ^ dr) * shards + (f ^ df)))
    with jax.named_scope(name):
        return lax.ppermute(rows, AXES, pairs)


HELD = (
    ((0, 0, 0), (0, 0, 1)),
    ((2, 0, 0), (1, 0, 1)),
    ((0, 1, 0), (0, 1, 1)),
    ((2, 0, 1), (1, 0, 0)),
    ((2, 1, 0), (1, 1, 1)),
    ((3, 0, 0), (3, 0, 1)),
    ((2, 1, 1), (1, 1, 0)),
    ((3, 1, 0), (3, 1, 1)),
)
SHARDS = (((0, 0), (2, 0)), ((1, 0), (3, 0)), ((0, 1), (2, 1)), ((1, 1), (3, 1)))


def position():
    x, f = lax.axis_index("rep"), lax.axis_index("fsdp")
    return x, f >> 1, f & 1


def flips_of(i, kind):
    first, second = HELD[i]
    return [a + kind * (b - a) for a, b in zip(first, second)]


def shard_of(flips):
    x, place, _ = position()
    return (place ^ (flips[0] * 2 + flips[1])) * 2 + (x ^ flips[2])


def update_kernel(replicas, old_ref, own_ref, oa_ref, ob_ref, ab_ref):
    rows_a = oa_ref.shape[1]
    ab_ref[:rows_a] = (old_ref[:rows_a] - step_size * ((own_ref[:rows_a] + oa_ref[0]) / replicas)).astype(jnp.bfloat16)
    ab_ref[rows_a:] = (old_ref[rows_a:] - step_size * ((own_ref[rows_a:] + ob_ref[0]) / replicas)).astype(jnp.bfloat16)


def weight_kernel(h_ref, hs_ref, *refs):
    *shard_refs, own_ref, other_ref, w_all = refs
    rows = shard_refs[0].shape[0]
    for i, ref in enumerate(shard_refs):
        w_all[i * rows : (i + 1) * rows] = ref[...]
    other_ref[...] = dot(hs_ref[...], w_all[...], NT)
    own_ref[...] = dot(h_ref[...], w_all[...], NT)


def place(block_of, rows, products, out):
    n, m = products.shape[1], out.shape[1]
    source = lax.broadcasted_iota(jnp.int32, (n, m), 0)
    target = lax.broadcasted_iota(jnp.int32, (n, m), 1)
    column = jnp.zeros((n, m), jnp.int32)
    for i, (held, kind) in enumerate(block_of):
        column = jnp.where(source // rows == i, shard_of(flips_of(held, kind)) * rows, column)
    columns = (target == column + source % rows).astype(jnp.bfloat16)
    for part in split_bf16(products):
        out = out + dot(part, columns, NN)
    return out


def split_bf16(v):
    high = v.astype(jnp.bfloat16)
    return high, (v - high.astype(jnp.float32)).astype(jnp.bfloat16)


def add_blocks(h_ref, w_ref, b_own, merged_ref, b_all, blocks, t):
    x, place, core = position()
    rows_b = w_ref.shape[0]
    rows_a = h_ref.shape[1] * rows_b // b_all.shape[0]
    for ref, other, at, first in blocks:
        for j, (dz, dy) in enumerate(SHARDS[at], first):
            shard = (place ^ (dz * 2 + dy)) * 2 + (core ^ other)
            row = j * (rows_a + rows_b)
            columns = pl.ds(pl.multiple_of(shard * rows_a, rows_a), rows_a)
            part = ref[row : row + rows_a]
            b_all[pl.ds(pl.multiple_of(shard * rows_b, rows_b), rows_b)] = ref[row + rows_a : row + rows_a + rows_b]
            t = t + dot(h_ref[:, columns], part, NN)
            merged_ref[:, columns] = (w_ref[:, columns].astype(jnp.float32) + dot(b_own, part, NT)).astype(jnp.bfloat16)
    return t


def middle_kernel(at, others, early, h_ref, w_ref, own_ref, received_ref, *refs):
    *ab_refs, t_ref, high_ref, merged_ref, b_all = refs
    x, place_at, core = position()
    kind = core ^ x
    rows_b = w_ref.shape[0]
    rows_a = h_ref.shape[1] * rows_b // b_all.shape[0]
    out = jnp.zeros(high_ref.shape, jnp.float32)
    for ref, which in ((own_ref, kind), (received_ref, 1 - kind)):
        out = place([(i, which) for i in range(early)], rows_b, ref[...], out)
    high_ref[...] = out
    b_own = ab_refs[0][rows_a : rows_a + rows_b]
    n = len(at)
    blocks = [(ref, 0, at[i], 0) for i, ref in enumerate(ab_refs[:n])]
    blocks += [(ref, 1, k, 0) for ref, k in zip(ab_refs[n:], others)]
    t_ref[...] = add_blocks(h_ref, w_ref, b_own, merged_ref, b_all, blocks, jnp.zeros(t_ref.shape, jnp.float32))


def late_kernel(late, h_ref, high_ref, *refs):
    *w_refs, out_ref = refs
    x, _, core = position()
    kind = core ^ x
    held = [(i, which) for which in (kind, 1 - kind) for i in late]
    products = dot(h_ref[...], jnp.concatenate([ref[...] for ref in w_refs]), NT)
    out_ref[...] = place(held, w_refs[0].shape[0], products, high_ref[...])


def last_kernel(at, h_ref, w_ref, t_ref, high_ref, m_ref, b_ref, first_ref, *refs):
    *ab_refs, out_ref, merged_ref, b_all = refs
    rows_b = w_ref.shape[0]
    rows_a = h_ref.shape[1] * rows_b // b_all.shape[0]
    b_own = first_ref[rows_a : rows_a + rows_b]
    merged_ref[...] = m_ref[...]
    b_all[...] = b_ref[...]
    own, joined = ab_refs
    blocks = [(own, 0, at[-1], 0)] + [(joined, 1, k, 2 * i) for i, k in enumerate(at)]
    t = add_blocks(h_ref, w_ref, b_own, merged_ref, b_all, blocks, t_ref[...])
    out = high_ref[...]
    for part in split_bf16(t):
        out = out + dot(part, b_all[...], NT)
    out_ref[...] = out.astype(jnp.bfloat16)


def cost(flops, number_of_bytes):
    return pl.CostEstimate(flops=int(flops), bytes_accessed=int(number_of_bytes), transcendentals=0)


def paired(hidden, weight, adapter_a, adapter_b, grad_a, grad_b):
    group = (lax.axis_size("rep"), lax.axis_size("fsdp"))
    tokens, depth = hidden.shape
    rank = adapter_a.shape[1]
    rows_a, rows_b = adapter_a.shape[0], weight.shape[0]
    outputs = rows_b * group[1]

    vmem = pl.BlockSpec(memory_space=pltpu.VMEM)
    params = pltpu.CompilerParams(vmem_limit_bytes=VMEM_LIMIT)
    bf16, f32 = jnp.bfloat16, jnp.float32

    hold = lax.optimization_barrier
    h_here, w_here = hidden, weight
    old = jnp.concatenate([adapter_a, adapter_b])
    mine = jnp.concatenate([grad_a[0], grad_b[0]])
    old, mine = hold((old, mine))
    w0 = weight
    other_a = send(grad_a, group, REPLICA, name="other_a")
    other_b = send(grad_b, group, REPLICA, name="other_b")
    w1 = send(w0, group, Z2, Z1, name="w1")
    w2 = send(w0, group, Y, name="w2")
    w1, w2 = hold((w1, w2))
    other_hidden = send(hidden, group, CORE, name="other_hidden")
    ab = pl.pallas_call(
        functools.partial(update_kernel, group[0]),
        out_shape=jax.ShapeDtypeStruct((rows_a + rows_b, rank), bf16),
        in_specs=[vmem] * 4,
        out_specs=vmem,
        compiler_params=params,
        cost_estimate=cost(U_FLOPS, 8 * rank * rows_a),
        name="update",
    )(old, mine, other_a, other_b)
    ab_far = send(ab, group, Z2, name="ab_far")
    w1, ab = hold((w1, ab))
    w3 = send(w1, group, X, name="w3")
    w4 = send(w1, group, Y, name="w4")
    w5 = send(w1, group, Z1, Z2, name="w5")
    ab_0 = jnp.concatenate([ab, ab_far])
    ab_1 = send(ab_0, group, Z1, name="ab_1")
    ab_2 = send(ab_0, group, Y, name="ab_2")
    other_0 = send(ab_0, group, CORE, name="other_0")
    ab_3 = send(ab_2, group, Z1, name="ab_3")
    w3, w4 = hold((w3, w4))
    w6 = send(w4, group, X, name="w6")
    w7 = send(w5, group, Y, name="w7")
    held = [w0, w1, w2, w3, w4, w5, w6, w7]
    other_2 = send(ab_2, group, CORE, name="other_2")
    joined = jnp.concatenate([ab_1, ab_3])
    other_3 = send(joined, group, CORE, name="other_3")
    ab_early = [ab_0, ab_1, ab_2, other_0, other_2]

    early = [w_here] + held[1:EARLY]
    late = held[EARLY:]
    early, other_0 = lax.optimization_barrier((early, other_0))
    ab_early = [ab_0, ab_1, ab_2, other_0, other_2]
    columns = rows_b * EARLY
    own, other = pl.pallas_call(
        weight_kernel,
        out_shape=[jax.ShapeDtypeStruct((tokens, columns), f32)] * 2,
        in_specs=[vmem] * (2 + EARLY),
        out_specs=[vmem] * 2,
        scratch_shapes=[pltpu.VMEM((columns, depth), bf16)],
        compiler_params=params,
        cost_estimate=cost(W_FLOPS * 4 * tokens * columns * depth, 2 * depth * (2 * tokens + columns)),
        name="weight_product",
    )(h_here, other_hidden, *early)
    received = send(other, group, CORE, name="received")
    middle = (0, 1, 2)
    t, high, merged, b_all = pl.pallas_call(
        functools.partial(middle_kernel, middle, (0, 2), EARLY),
        out_shape=[
            jax.ShapeDtypeStruct((tokens, rank), f32),
            jax.ShapeDtypeStruct((tokens, outputs), f32),
            jax.ShapeDtypeStruct(weight.shape, bf16),
            jax.ShapeDtypeStruct((outputs, rank), bf16),
        ],
        in_specs=[vmem] * (4 + len(ab_early)),
        out_specs=[vmem] * 4,
        compiler_params=params,
        cost_estimate=cost(M_FLOPS * 2 * tokens * rank * depth, 2 * depth * (tokens + rank)),
        name="middle",
    )(h_here, w_here, own, received, *ab_early)
    late, t = lax.optimization_barrier((late, t))
    other_late = [send(v, group, CORE, name="other_late") for v in late]
    high = pl.pallas_call(
        functools.partial(late_kernel, tuple(range(EARLY, len(HELD)))),
        out_shape=jax.ShapeDtypeStruct((tokens, outputs), f32),
        in_specs=[vmem] * (2 + 2 * len(late)),
        out_specs=vmem,
        compiler_params=params,
        cost_estimate=cost(L_FLOPS, 2 * outputs * tokens),
        name="late_product",
    )(h_here, high, *late, *other_late)
    return tuple(pl.pallas_call(
        functools.partial(last_kernel, (1, 3)),
        out_shape=[
            jax.ShapeDtypeStruct((tokens, outputs), bf16),
            jax.ShapeDtypeStruct(weight.shape, bf16),
        ],
        in_specs=[vmem] * 9,
        out_specs=[vmem] * 2,
        scratch_shapes=[pltpu.VMEM((outputs, rank), bf16)],
        compiler_params=params,
        cost_estimate=cost(2 * tokens * rank * outputs, 2 * outputs * tokens),
        name="last",
    )(h_here, w_here, t, high, merged, b_all, ab_0, ab_3, other_3))


def solution(mesh):
    paired_fits = mesh.shape["rep"] == 2 and mesh.shape["fsdp"] == 16
    return jax.shard_map(
        paired if paired_fits else general,
        mesh=mesh,
        in_specs=(
            P(("rep", "fsdp"), None),
            P("fsdp", None),
            P("fsdp", None),
            P("fsdp", None),
            P("rep", "fsdp", None),
            P("rep", "fsdp", None),
        ),
        out_specs=(P(("rep", "fsdp"), None), P("fsdp", None)),
        check_vma=False,
    )
```

```python
import functools

import jax
import jax.numpy as jnp
from jax import lax
from jax.experimental import pallas as pl
from jax.experimental.pallas import tpu as pltpu
from jax.sharding import PartitionSpec as P

step_size = 0.5
AXES = ("rep", "fsdp")
NT = (((1,), (1,)), ((), ()))
NN = (((1,), (0,)), ((), ()))
VMEM_LIMIT = 8 * 1024 * 1024
EARLY = 6
U_FLOPS = 4e9
L_FLOPS = 1e9
W_FLOPS = 4
M_FLOPS = 1


def dot(a, b, dims):
    return lax.dot_general(a, b, dims, preferred_element_type=jnp.float32)


def general(hidden, weight, adapter_a, adapter_b, grad_a, grad_b):
    replicas = lax.axis_size("rep")
    summed = lax.psum((grad_a[0], grad_b[0]), "rep")
    new_a = adapter_a - step_size * (summed[0] / replicas)
    new_b = adapter_b - step_size * (summed[1] / replicas)
    full_a = lax.all_gather(new_a, "fsdp", axis=0, tiled=True)
    delta = lax.dot_general(new_b, full_a, NT, precision=lax.Precision.HIGHEST, preferred_element_type=jnp.float32)
    own_rows = (weight.astype(jnp.float32) + delta).astype(jnp.bfloat16)
    output = dot(hidden, lax.all_gather(own_rows, "fsdp", axis=0, tiled=True), NT)
    return output.astype(jnp.bfloat16), own_rows


CORE, Y, Z1, Z2 = (0, 1), (0, 2), (0, 4), (0, 8)
REPLICA, X = (1, 0), (1, 1)


def send(rows, group, move, other_move=None, name="sent"):
    reps, shards = group
    pairs = []
    for r in range(reps):
        for f in range(shards):
            dr, df = move if (f & 1) == r or other_move is None else other_move
            pairs.append((r * shards + f, (r ^ dr) * shards + (f ^ df)))
    with jax.named_scope(name):
        return lax.ppermute(rows, AXES, pairs)


HELD = (
    ((0, 0, 0), (0, 0, 1)),
    ((2, 0, 0), (1, 0, 1)),
    ((0, 1, 0), (0, 1, 1)),
    ((2, 0, 1), (1, 0, 0)),
    ((2, 1, 0), (1, 1, 1)),
    ((3, 0, 0), (3, 0, 1)),
    ((2, 1, 1), (1, 1, 0)),
    ((3, 1, 0), (3, 1, 1)),
)
SHARDS = (((0, 0), (2, 0)), ((1, 0), (3, 0)), ((0, 1), (2, 1)), ((1, 1), (3, 1)))


def position():
    x, f = lax.axis_index("rep"), lax.axis_index("fsdp")
    return x, f >> 1, f & 1


def flips_of(i, kind):
    first, second = HELD[i]
    return [a + kind * (b - a) for a, b in zip(first, second)]


def shard_of(flips):
    x, place, _ = position()
    return (place ^ (flips[0] * 2 + flips[1])) * 2 + (x ^ flips[2])


def update_kernel(replicas, old_ref, own_ref, oa_ref, ob_ref, ab_ref):
    rows_a = oa_ref.shape[1]
    ab_ref[:rows_a] = (old_ref[:rows_a] - step_size * ((own_ref[:rows_a] + oa_ref[0]) / replicas)).astype(jnp.bfloat16)
    ab_ref[rows_a:] = (old_ref[rows_a:] - step_size * ((own_ref[rows_a:] + ob_ref[0]) / replicas)).astype(jnp.bfloat16)


def weight_kernel(h_ref, hs_ref, *refs):
    *shard_refs, own_ref, other_ref, w_all = refs
    rows = shard_refs[0].shape[0]
    for i, ref in enumerate(shard_refs):
        w_all[i * rows : (i + 1) * rows] = ref[...]
    other_ref[...] = dot(hs_ref[...], w_all[...], NT)
    own_ref[...] = dot(h_ref[...], w_all[...], NT)


def place(block_of, rows, products, out):
    n, m = products.shape[1], out.shape[1]
    source = lax.broadcasted_iota(jnp.int32, (n, m), 0)
    target = lax.broadcasted_iota(jnp.int32, (n, m), 1)
    column = jnp.zeros((n, m), jnp.int32)
    for i, (held, kind) in enumerate(block_of):
        column = jnp.where(source // rows == i, shard_of(flips_of(held, kind)) * rows, column)
    columns = (target == column + source % rows).astype(jnp.bfloat16)
    both = jnp.concatenate(split_bf16(products), axis=1)
    return out + dot(both, jnp.concatenate([columns, columns]), NN)


def split_bf16(v):
    high = v.astype(jnp.bfloat16)
    return high, (v - high.astype(jnp.float32)).astype(jnp.bfloat16)


def add_blocks(h_ref, w_ref, b_own, merged_ref, b_all, blocks, t):
    x, place, core = position()
    rows_b = w_ref.shape[0]
    rows_a = h_ref.shape[1] * rows_b // b_all.shape[0]
    for ref, other, at, first in blocks:
        for j, (dz, dy) in enumerate(SHARDS[at], first):
            shard = (place ^ (dz * 2 + dy)) * 2 + (core ^ other)
            row = j * (rows_a + rows_b)
            columns = pl.ds(pl.multiple_of(shard * rows_a, rows_a), rows_a)
            part = ref[row : row + rows_a]
            b_all[pl.ds(pl.multiple_of(shard * rows_b, rows_b), rows_b)] = ref[row + rows_a : row + rows_a + rows_b]
            t = t + dot(h_ref[:, columns], part, NN)
            merged_ref[:, columns] = (w_ref[:, columns].astype(jnp.float32) + dot(b_own, part, NT)).astype(jnp.bfloat16)
    return t


def middle_kernel(at, others, early, h_ref, w_ref, own_ref, received_ref, *refs):
    *ab_refs, t_ref, high_ref, merged_ref, b_all = refs
    x, place_at, core = position()
    kind = core ^ x
    rows_b = w_ref.shape[0]
    rows_a = h_ref.shape[1] * rows_b // b_all.shape[0]
    out = jnp.zeros(high_ref.shape, jnp.float32)
    for ref, which in ((own_ref, kind), (received_ref, 1 - kind)):
        out = place([(i, which) for i in range(early)], rows_b, ref[...], out)
    high_ref[...] = out
    b_own = ab_refs[0][rows_a : rows_a + rows_b]
    n = len(at)
    blocks = [(ref, 0, at[i], 0) for i, ref in enumerate(ab_refs[:n])]
    blocks += [(ref, 1, k, 0) for ref, k in zip(ab_refs[n:], others)]
    t_ref[...] = add_blocks(h_ref, w_ref, b_own, merged_ref, b_all, blocks, jnp.zeros(t_ref.shape, jnp.float32))


def late_kernel(late, h_ref, high_ref, *refs):
    *w_refs, out_ref = refs
    x, _, core = position()
    kind = core ^ x
    held = [(i, which) for which in (kind, 1 - kind) for i in late]
    products = dot(h_ref[...], jnp.concatenate([ref[...] for ref in w_refs]), NT)
    out_ref[...] = place(held, w_refs[0].shape[0], products, high_ref[...])


def last_kernel(at, h_ref, w_ref, t_ref, high_ref, m_ref, b_ref, first_ref, *refs):
    *ab_refs, out_ref, merged_ref, b_all = refs
    rows_b = w_ref.shape[0]
    rows_a = h_ref.shape[1] * rows_b // b_all.shape[0]
    b_own = first_ref[rows_a : rows_a + rows_b]
    merged_ref[...] = m_ref[...]
    b_all[...] = b_ref[...]
    own, joined = ab_refs
    blocks = [(own, 0, at[-1], 0)] + [(joined, 1, k, 2 * i) for i, k in enumerate(at)]
    t = add_blocks(h_ref, w_ref, b_own, merged_ref, b_all, blocks, t_ref[...])
    both = jnp.concatenate(split_bf16(t), axis=1)
    out = high_ref[...] + dot(both, jnp.concatenate([b_all[...], b_all[...]], axis=1), NT)
    out_ref[...] = out.astype(jnp.bfloat16)


def cost(flops, number_of_bytes):
    return pl.CostEstimate(flops=int(flops), bytes_accessed=int(number_of_bytes), transcendentals=0)


def paired(hidden, weight, adapter_a, adapter_b, grad_a, grad_b):
    group = (lax.axis_size("rep"), lax.axis_size("fsdp"))
    tokens, depth = hidden.shape
    rank = adapter_a.shape[1]
    rows_a, rows_b = adapter_a.shape[0], weight.shape[0]
    outputs = rows_b * group[1]

    vmem = pl.BlockSpec(memory_space=pltpu.VMEM)
    params = pltpu.CompilerParams(vmem_limit_bytes=VMEM_LIMIT)
    bf16, f32 = jnp.bfloat16, jnp.float32

    hold = lax.optimization_barrier
    h_here, w_here = hidden, weight
    old = jnp.concatenate([adapter_a, adapter_b])
    mine = jnp.concatenate([grad_a[0], grad_b[0]])
    old, mine = hold((old, mine))
    w0 = weight
    other_a = send(grad_a, group, REPLICA, name="other_a")
    other_b = send(grad_b, group, REPLICA, name="other_b")
    w1 = send(w0, group, Z2, Z1, name="w1")
    w2 = send(w0, group, Y, name="w2")
    w1, w2 = hold((w1, w2))
    other_hidden = send(hidden, group, CORE, name="other_hidden")
    ab = pl.pallas_call(
        functools.partial(update_kernel, group[0]),
        out_shape=jax.ShapeDtypeStruct((rows_a + rows_b, rank), bf16),
        in_specs=[vmem] * 4,
        out_specs=vmem,
        compiler_params=params,
        cost_estimate=cost(U_FLOPS, 8 * rank * rows_a),
        name="update",
    )(old, mine, other_a, other_b)
    ab_far = send(ab, group, Z2, name="ab_far")
    w1, ab = hold((w1, ab))
    w3 = send(w1, group, X, name="w3")
    w4 = send(w1, group, Y, name="w4")
    w5 = send(w1, group, Z1, Z2, name="w5")
    ab_0 = jnp.concatenate([ab, ab_far])
    ab_1 = send(ab_0, group, Z1, name="ab_1")
    ab_2 = send(ab_0, group, Y, name="ab_2")
    other_0 = send(ab_0, group, CORE, name="other_0")
    ab_3 = send(ab_2, group, Z1, name="ab_3")
    w3, w4 = hold((w3, w4))
    w6 = send(w4, group, X, name="w6")
    w7 = send(w5, group, Y, name="w7")
    held = [w0, w1, w2, w3, w4, w5, w6, w7]
    other_2 = send(ab_2, group, CORE, name="other_2")
    joined = jnp.concatenate([ab_1, ab_3])
    other_3 = send(joined, group, CORE, name="other_3")
    ab_early = [ab_0, ab_1, ab_2, other_0, other_2]

    early = [w_here] + held[1:EARLY]
    late = held[EARLY:]
    early, other_0 = lax.optimization_barrier((early, other_0))
    ab_early = [ab_0, ab_1, ab_2, other_0, other_2]
    columns = rows_b * EARLY
    own, other = pl.pallas_call(
        weight_kernel,
        out_shape=[jax.ShapeDtypeStruct((tokens, columns), f32)] * 2,
        in_specs=[vmem] * (2 + EARLY),
        out_specs=[vmem] * 2,
        scratch_shapes=[pltpu.VMEM((columns, depth), bf16)],
        compiler_params=params,
        cost_estimate=cost(W_FLOPS * 4 * tokens * columns * depth, 2 * depth * (2 * tokens + columns)),
        name="weight_product",
    )(h_here, other_hidden, *early)
    received = send(other, group, CORE, name="received")
    middle = (0, 1, 2)
    t, high, merged, b_all = pl.pallas_call(
        functools.partial(middle_kernel, middle, (0, 2), EARLY),
        out_shape=[
            jax.ShapeDtypeStruct((tokens, rank), f32),
            jax.ShapeDtypeStruct((tokens, outputs), f32),
            jax.ShapeDtypeStruct(weight.shape, bf16),
            jax.ShapeDtypeStruct((outputs, rank), bf16),
        ],
        in_specs=[vmem] * (4 + len(ab_early)),
        out_specs=[vmem] * 4,
        compiler_params=params,
        cost_estimate=cost(M_FLOPS * 2 * tokens * rank * depth, 2 * depth * (tokens + rank)),
        name="middle",
    )(h_here, w_here, own, received, *ab_early)
    late, t = lax.optimization_barrier((late, t))
    other_late = [send(v, group, CORE, name="other_late") for v in late]
    high = pl.pallas_call(
        functools.partial(late_kernel, tuple(range(EARLY, len(HELD)))),
        out_shape=jax.ShapeDtypeStruct((tokens, outputs), f32),
        in_specs=[vmem] * (2 + 2 * len(late)),
        out_specs=vmem,
        compiler_params=params,
        cost_estimate=cost(L_FLOPS, 2 * outputs * tokens),
        name="late_product",
    )(h_here, high, *late, *other_late)
    return tuple(pl.pallas_call(
        functools.partial(last_kernel, (1, 3)),
        out_shape=[
            jax.ShapeDtypeStruct((tokens, outputs), bf16),
            jax.ShapeDtypeStruct(weight.shape, bf16),
        ],
        in_specs=[vmem] * 9,
        out_specs=[vmem] * 2,
        scratch_shapes=[pltpu.VMEM((outputs, rank), bf16)],
        compiler_params=params,
        cost_estimate=cost(2 * tokens * rank * outputs, 2 * outputs * tokens),
        name="last",
    )(h_here, w_here, t, high, merged, b_all, ab_0, ab_3, other_3))


def solution(mesh):
    paired_fits = mesh.shape["rep"] == 2 and mesh.shape["fsdp"] == 16
    return jax.shard_map(
        paired if paired_fits else general,
        mesh=mesh,
        in_specs=(
            P(("rep", "fsdp"), None),
            P("fsdp", None),
            P("fsdp", None),
            P("fsdp", None),
            P("rep", "fsdp", None),
            P("rep", "fsdp", None),
        ),
        out_specs=(P(("rep", "fsdp"), None), P("fsdp", None)),
        check_vma=False,
    )
```
